256 devices in a mesh: sp: 16 (over z, core), fsdp: 16 (over x, y).
Axes of the slice: x: 4, y: 4, z: 8, core: 2. Of those that a mesh axis runs over, the one named last changes fastest.
Arguments:
- x_video: bfloat16 [16, 1024, 3072], P('fsdp', 'sp'), may hold values from -6 to 6
- x_audio: bfloat16 [16, 1024, 3072], P('fsdp', 'sp'), may hold values from -6 to 6
- len_video: int32 [16], P('fsdp'), may hold values from 256 to 1024, as said below
- len_audio: int32 [16], P('fsdp'), may hold values from 256 to 1024, as said below
- in_video: bfloat16 [3072, 6, 2048], P('fsdp', None, 'sp'), may hold values from -0.68560344 to 0.68560344
- in_audio: bfloat16 [3072, 6, 2048], P('fsdp', None, 'sp'), may hold values from -0.68560344 to 0.68560344
- out_video: bfloat16 [2, 2048, 3072], P(None, 'sp', 'fsdp'), may hold values from -0.375 to 0.375
- out_audio: bfloat16 [2, 2048, 3072], P(None, 'sp', 'fsdp'), may hold values from -0.375 to 0.375
Outputs:
- y_video: float32 [16, 1024, 3072], P('fsdp', 'sp')
- y_audio: float32 [16, 1024, 3072], P('fsdp', 'sp')
The draws below stay inside these ranges and needn't reach their ends.
Inputs may be any that keep to these rules, and one draw needn't show every extreme that they name: `len_video`: valid video tokens of a clip; some clip has all 1024 and some clip 1024 // 4. `len_audio`: valid audio tokens of a clip; some clip has all 1024 and some clip 1024 // 4.
All inputs are finite; a program needn't handle non-finite values.
Results may differ from the reference program's by a relative error of at most 0.0032.
Values may be sent and summed in bfloat16 or wider, within the bound.
No kernel may reach another device: no remote copies, remote signals or barrier semaphores. Data moves between devices by JAX's collectives and lax.ppermute only.
A program may use at most 128 MiB of HBM per device.

```python
import jax
import jax.numpy as jnp
from jax import lax

D = 3072
HEADS = 16
HDIM = 128
TV = 1024
TA = 1024
CLIPS = 16
INNER = 2048
N_SP = 16


def spread_lengths(key, total, count):
    key_vals, key_first, key_second = jax.random.split(key, 3)
    values = jax.random.randint(key_vals, (count,), total // 4, total + 1)
    first = jax.random.randint(key_first, (), 0, count)
    second = (first + 1 + jax.random.randint(key_second, (), 0, count - 1)) % count
    places = jnp.arange(count)
    values = jnp.where(places == first, total, values)
    values = jnp.where(places == second, total // 4, values)
    return values.astype(jnp.int32)


def video_lengths(key):
    return spread_lengths(jax.random.fold_in(key, 11), TV, CLIPS)


def audio_lengths(key):
    return spread_lengths(jax.random.fold_in(key, 23), TA, CLIPS)


def shared_parts(key):
    direction = jnp.clip(jax.random.normal(jax.random.fold_in(key, 5), (D,), jnp.float32), -3.0, 3.0)
    shared_block = jnp.clip(jax.random.normal(jax.random.fold_in(key, 7), (D, HDIM), jnp.float32), -3.0, 3.0) * D ** (-0.5)
    chosen = jax.random.randint(jax.random.fold_in(key, 9), (), 0, HEADS)
    return (direction, shared_block, chosen)


def place_tokens(direction, lengths, rough_part, common, total):
    positions = jnp.arange(total)
    side_sign = jnp.where(positions[None, :] < lengths[:, None], 1.0, -1.0).astype(jnp.float32)
    return common * side_sign[:, :, None] * direction[None, None, :] + rough_part


def plant_block(plain_part, shared_block, chosen, boost_scale):
    column = (jnp.arange(INNER) // HDIM == chosen).astype(jnp.float32)
    slot_mask = jnp.array([1.0, 1.0, 0.0, 1.0, 1.0, 0.0], jnp.float32)
    tiled_block = jnp.tile(shared_block, (1, HEADS))
    planted = boost_scale * tiled_block[:, None, :] * slot_mask[None, :, None] * column[None, None, :]
    return plain_part + planted


def token_draw(key, lengths, direction, total, salt):
    key = jax.random.fold_in(key, salt)
    key_rough = jax.random.fold_in(key, 0)
    rough_part = jnp.clip(jax.random.normal(key_rough, (CLIPS, total, D), jnp.float32), -4.5, 4.5)
    common = 0.4
    return place_tokens(direction, lengths, rough_part, common, total).astype(jnp.bfloat16)


def weight_draw(key, shared_block, chosen, salt):
    key = jax.random.fold_in(key, salt)
    plain_part = jnp.clip(jax.random.normal(key, (D, 6, INNER), jnp.float32), -3.0, 3.0) * D ** (-0.5)
    boost_scale = 1.5
    return plant_block(plain_part, shared_block, chosen, boost_scale).astype(jnp.bfloat16)


def draw_len_video(key, part):
    return video_lengths(key)


def draw_len_audio(key, part):
    return audio_lengths(key)


def draw_x_video(key, part):
    direction, shared_block, chosen = shared_parts(key)
    lengths = video_lengths(key)
    return token_draw(key, lengths, direction, TV, 31)


def draw_x_audio(key, part):
    direction, shared_block, chosen = shared_parts(key)
    lengths = audio_lengths(key)
    return token_draw(key, lengths, direction, TA, 37)


def draw_in_video(key, part):
    direction, shared_block, chosen = shared_parts(key)
    return weight_draw(key, shared_block, chosen, 41)


def draw_in_audio(key, part):
    direction, shared_block, chosen = shared_parts(key)
    return weight_draw(key, shared_block, chosen, 43)


def level_of(rng, dims, pieces, least, largest):
    loudness = 1.0
    for position, blocks in pieces:
        heights = jax.random.uniform(jax.random.fold_in(jax.random.fold_in(rng, 6), position), (blocks,), jnp.float32, least / len(pieces), largest / len(pieces))
        loudness = loudness * jnp.repeat(jnp.exp(heights), dims[position] // blocks).reshape((-1,) + (1,) * (len(dims) - 1 - position))
    return loudness


def centred(rng, shape, scale, bound, shards=(), kind=jnp.bfloat16):
    values = jax.random.normal(rng, shape, jnp.float32) * scale
    if len(shards) > 0:
        values = level_of(rng, shape, shards, -0.22, 0.18) * values
    return jnp.clip(values, min=-bound, max=bound).astype(kind)


def setup_inputs(seed: int = 0) -> dict:
    keys = jax.random.split(jax.random.key(seed), 9)
    x_video = draw_x_video(jax.random.fold_in(keys[8], 71), 0)
    x_audio = draw_x_audio(jax.random.fold_in(keys[8], 71), 0)
    len_video = draw_len_video(jax.random.fold_in(keys[8], 71), 0)
    len_audio = draw_len_audio(jax.random.fold_in(keys[8], 71), 0)
    in_video = draw_in_video(jax.random.fold_in(keys[8], 71), 0)
    in_audio = draw_in_audio(jax.random.fold_in(keys[8], 71), 0)
    out_video = centred(keys[6], (2, INNER, D), (INNER // 8) ** -0.5, 0.375, ((1, 16), (2, 16)))
    out_audio = centred(keys[7], (2, INNER, D), (INNER // 8) ** -0.5, 0.375, ((1, 16), (2, 16)))
    return {"x_video": x_video, "x_audio": x_audio, "len_video": len_video, "len_audio": len_audio, "in_video": in_video, "in_audio": in_audio, "out_video": out_video, "out_audio": out_audio}


EPS = 1e-06

def layer_norm(x):
    values = x.astype(jnp.float32)
    centre = lax.optimization_barrier(jnp.mean(values, axis=-1, keepdims=True))
    spread = lax.optimization_barrier(jnp.mean((values - centre) ** 2, axis=-1, keepdims=True))
    return ((values - centre) * lax.rsqrt(spread + EPS)).astype(jnp.bfloat16)

def normalize(proj):
    inner = proj.shape[2]
    factors = []
    for slot in range(6):
        if slot in (2, 5):
            factors.append(jnp.ones((proj.shape[0],), jnp.float32))
        else:
            total = lax.optimization_barrier(jnp.sum(proj[:, slot] * proj[:, slot], axis=-1))
            factors.append(lax.rsqrt(total / inner + EPS))
    scales = jnp.stack(factors, axis=1)
    return (proj * scales[:, :, None]).astype(jnp.bfloat16)

def attend(query, key, value, length):
    heads = query.shape[1] // HDIM
    q_rows = query.reshape(query.shape[0], heads, HDIM).astype(jnp.float32)
    k_rows = key.reshape(key.shape[0], heads, HDIM).astype(jnp.float32)
    v_rows = value.reshape(value.shape[0], heads, HDIM).astype(jnp.float32)
    scores = jnp.einsum('qhd,khd->hqk', q_rows, k_rows) * HDIM ** (-0.5)
    valid = jnp.arange(key.shape[0], dtype=jnp.int32) < length
    scores = jnp.where(valid[None, None, :], scores, -1e+30)
    top = lax.optimization_barrier(jnp.max(scores, axis=-1, keepdims=True))
    expo = jnp.exp(scores - top)
    weights = (expo / lax.optimization_barrier(jnp.sum(expo, axis=-1, keepdims=True))).astype(jnp.bfloat16)
    result = jnp.einsum('hqk,khd->qhd', weights.astype(jnp.float32), v_rows)
    return result.astype(jnp.bfloat16).reshape(query.shape[0], heads * HDIM)

def combine(tokens, attended, weight):
    groups = N_SP
    rows = attended.shape[1]
    width = attended.shape[2] // groups
    parts = attended.reshape(2, rows, groups, width).astype(jnp.float32)
    mats = weight.reshape(2, groups, width, weight.shape[2]).astype(jnp.float32)
    partial_value = jnp.einsum('stgi,sgie->gte', parts, mats)
    summed = lax.optimization_barrier(jnp.sum(partial_value, axis=0))
    return tokens.astype(jnp.float32) + summed

def reference(x_video, x_audio, len_video, len_audio, in_video, in_audio, out_video, out_audio):
    wide_in_v = in_video.astype(jnp.float32)
    wide_in_a = in_audio.astype(jnp.float32)

    def one_clip(items):
        tok_v, tok_a, size_v, size_a = items
        proj_v = jnp.einsum('td,dsh->tsh', layer_norm(tok_v).astype(jnp.float32), wide_in_v)
        proj_a = jnp.einsum('td,dsh->tsh', layer_norm(tok_a).astype(jnp.float32), wide_in_a)
        qkv_v = normalize(proj_v)
        qkv_a = normalize(proj_a)
        att_v = jnp.stack([attend(qkv_v[:, 0], qkv_v[:, 1], qkv_v[:, 2], size_v), attend(qkv_v[:, 3], qkv_a[:, 4], qkv_a[:, 5], size_a)])
        att_a = jnp.stack([attend(qkv_a[:, 0], qkv_a[:, 1], qkv_a[:, 2], size_a), attend(qkv_a[:, 3], qkv_v[:, 4], qkv_v[:, 5], size_v)])
        return (combine(tok_v, att_v, out_video), combine(tok_a, att_a, out_audio))
    y_video, y_audio = lax.map(one_clip, (x_video, x_audio, len_video, len_audio))
    return (y_video, y_audio)
```

```python
import functools

import jax
import jax.numpy as jnp
from jax import lax
from jax.experimental import pallas as pl
from jax.experimental.pallas import tpu as pltpu
from jax.sharding import PartitionSpec as P

HDIM = 128
INNER = 2048
EPS = 1e-06
CHIPS = 8
ROWS = 192
LOG2E = 1.4426950408889634
NEAR = (0, 7, 1, 6, 2, 5, 3)
VMEM_BYTES = 56 * 1024 * 1024


def along_z(value, step):
    return lax.ppermute(value, "sp", [(s, ((s // 2 + step) % CHIPS) * 2 + s % 2) for s in range(16)])


def other_core(value):
    return lax.ppermute(value, "sp", [(s, s ^ 1) for s in range(16)])


def along_x(value, step):
    return lax.ppermute(value, "fsdp", [(f, ((f // 4 + step) % 4) * 4 + f % 4) for f in range(16)])


def along_y(value, step):
    return lax.ppermute(value, "fsdp", [(f, f // 4 * 4 + (f % 4 + step) % 4) for f in range(16)])


def norm_kernel(video_ref, audio_ref, out_ref):
    for at, ref in enumerate((video_ref, audio_ref)):
        values = ref[...].astype(jnp.float32)
        centre = jnp.mean(values, axis=-1, keepdims=True)
        values = values - centre
        spread = jnp.mean(values * values, axis=-1, keepdims=True)
        out_ref[pl.ds(64 * at, 64), :] = (values * lax.rsqrt(spread + EPS)).astype(jnp.bfloat16)


def layer_norms(video, audio):
    return pl.pallas_call(
        norm_kernel,
        out_shape=jax.ShapeDtypeStruct((128, 3072), jnp.bfloat16),
        cost_estimate=pl.CostEstimate(flops=128 * 3072 * 8, bytes_accessed=128 * 3072 * 4, transcendentals=128),
        name="layer_norms",
    )(video, audio)


def gather_tokens(own):
    blocks = {0: own}
    ahead, behind = own, own
    for step in (1, 2, 3):
        ahead, behind = along_z(ahead, 1), along_z(behind, -1)
        blocks[CHIPS - step], blocks[step] = ahead, behind
    rows = own.shape[0] // 2
    return blocks, along_z(ahead[:rows], 1), along_z(behind[rows:], -1)


def gather_plane(own):
    up, down = along_y(own, 1), along_y(own, -1)
    half = own.shape[0] // 2
    far = jnp.concatenate([along_y(up[:half], 1), along_y(down[half:], -1)])
    line = jnp.stack([own, up, far, down])
    up, down = along_x(line, 1), along_x(line, -1)
    return line, up, down, along_x(up[:2], 1), along_x(down[2:], -1)


def project_kernel(row_ref, *refs):
    near, far, wide, pieces = refs[:14], refs[14:18], refs[18], refs[19:24]
    out_ref, square_ref, x_buf, w_buf, x_sem, w_sem = refs[24:]
    for tower in (0, 1):
        half = pl.ds(64 * tower, 64)
        for core in (0, 1):
            for at, place in enumerate(NEAR):
                row = pl.multiple_of(row_ref[2 * place + core], 64)
                pltpu.make_async_copy(
                    near[2 * at + core].at[half], x_buf.at[tower, pl.ds(row, 64)], x_sem.at[tower]
                ).start()
            row = pl.multiple_of(row_ref[8 + core], 64)
            pltpu.make_async_copy(
                far[2 * tower + core], x_buf.at[tower, pl.ds(row, 64)], x_sem.at[tower]
            ).start()
        if tower == 0:
            pltpu.make_async_copy(wide.at[pl.ds(0, 6)], w_buf.at[0], w_sem.at[0]).start()
        else:
            for place in range(16):
                row = pl.multiple_of(row_ref[16 + place], 64)
                group, inner = place // 4, place % 4
                if group == 3:
                    group, inner = (3, inner) if inner < 2 else (4, inner - 2)
                pltpu.make_async_copy(
                    pieces[group].at[inner], w_buf.at[1, :, pl.ds(row, ROWS)], w_sem.at[1]
                ).start()
    for tower in (0, 1):
        pltpu.make_async_copy(x_buf.at[tower], x_buf.at[tower], x_sem.at[tower]).wait()
        pltpu.make_async_copy(w_buf.at[tower], w_buf.at[tower], w_sem.at[tower]).wait()

        def tile(m, _):
            rows = pl.ds(pl.multiple_of(m * 512, 512), 512)
            total = None
            for k in range(0, 3072, 512):
                weights = jnp.concatenate([w_buf[tower, slot, k : k + 512] for slot in range(6)], axis=1)
                term = jnp.dot(x_buf[tower, rows, k : k + 512], weights, preferred_element_type=jnp.float32)
                total = term if total is None else total + term
            for slot in range(6):
                part = total[:, 128 * slot : 128 * slot + 128]
                out_ref[tower, slot, rows, :] = part
                if slot not in (2, 5):
                    line = 4 * tower + (0, 1, 0, 2, 3)[slot]
                    square_ref[line : line + 1, rows] = jnp.sum(
                        jnp.transpose(part * part), axis=0, keepdims=True
                    )
            return 0

        lax.fori_loop(0, 2, tile, 0)


def project(rows, near, far, wide, pieces):
    return pl.pallas_call(
        project_kernel,
        in_specs=[pl.BlockSpec(memory_space=pltpu.SMEM)] + [pl.BlockSpec(memory_space=pl.ANY)] * 24,
        scratch_shapes=[
            pltpu.VMEM((2, 1024, 3072), jnp.bfloat16),
            pltpu.VMEM((2, 6, 3072, 128), jnp.bfloat16),
            pltpu.SemaphoreType.DMA((2,)),
            pltpu.SemaphoreType.DMA((2,)),
        ],
        out_shape=[
            jax.ShapeDtypeStruct((2, 6, 1024, 128), jnp.float32),
            jax.ShapeDtypeStruct((8, 1024), jnp.float32),
        ],
        compiler_params=pltpu.CompilerParams(vmem_limit_bytes=VMEM_BYTES),
        cost_estimate=pl.CostEstimate(flops=9663676416, bytes_accessed=28000000, transcendentals=0),
        name="project",
    )(rows, *near, *far, wide, *pieces)


def over_heads(local):
    pair = local + other_core(local)
    two = pair + along_z(pair, 1)
    three = two + along_z(pair, -1)
    return three + along_z(three, 3) + along_z(two, -3)


def attend_block(query_ref, key_ref, value_ref, rows, put):
    for tower in (0, 1):
        for kind in (0, 1):
            other = tower ^ kind
            scores = lax.dot_general(
                query_ref[tower, kind, rows, :],
                key_ref[other, kind],
                (((1,), (1,)), ((), ())),
                preferred_element_type=jnp.float32,
            )
            top = jnp.max(scores, axis=-1, keepdims=True)
            expo = jnp.exp2((scores - top) * (LOG2E * HDIM ** (-0.5))).astype(jnp.bfloat16)
            result = jnp.dot(expo, value_ref[other, kind], preferred_element_type=jnp.float32)
            put(tower, kind, (result[:, :128] / result[:, 128:]).astype(jnp.bfloat16))


def split_block(value, core):
    low, high = value[:64], value[64:]
    return jnp.where(core == 0, low, high), jnp.where(core == 0, high, low)


def first_kernel(place_ref, proj_ref, total_ref, query_ref, key_ref, value_ref, own_ref, other_ref):
    scales = jnp.transpose(lax.rsqrt(total_ref[...] / INNER + EPS))
    lane = lax.broadcasted_iota(jnp.int32, (1024, 128), 1)
    row = lax.broadcasted_iota(jnp.int32, (1024, 128), 0)
    one = jnp.where(lane == 0, 1.0, 0.0).astype(jnp.bfloat16)
    for tower in (0, 1):
        past = (lane == 0) & (row >= place_ref[2 + tower])
        mask = jnp.where(past, -1e30, 0.0).astype(jnp.bfloat16)
        for kind in (0, 1):
            line = 4 * tower + 2 * kind
            query = proj_ref[tower, 3 * kind] * scales[:, line : line + 1]
            key = proj_ref[tower, 3 * kind + 1] * scales[:, line + 1 : line + 2]
            query_ref[tower, kind, :, :128] = query.astype(jnp.bfloat16)
            query_ref[tower, kind, :, 128:] = one
            key_ref[tower, kind, :, :128] = key.astype(jnp.bfloat16)
            key_ref[tower, kind, :, 128:] = mask
            value_ref[tower, kind, :, :128] = proj_ref[tower, 3 * kind + 2].astype(jnp.bfloat16)
            value_ref[tower, kind, :, 128:] = jnp.ones((1024, 128), jnp.bfloat16)

    def put(tower, kind, value):
        lanes = pl.ds(128 * kind, 128)
        own_ref[tower, :, lanes], other_ref[tower, :, lanes] = split_block(value, place_ref[1])

    rows = pl.ds(pl.multiple_of(lax.rem(place_ref[0] + 4, CHIPS) * 128, 128), 128)
    attend_block(query_ref, key_ref, value_ref, rows, put)


def attend_first(place, proj, totals):
    block = jax.ShapeDtypeStruct((2, 64, 256), jnp.bfloat16)
    wide = jax.ShapeDtypeStruct((2, 2, 1024, 256), jnp.bfloat16)
    return pl.pallas_call(
        first_kernel,
        in_specs=[pl.BlockSpec(memory_space=pltpu.SMEM)] + [pl.BlockSpec(memory_space=pltpu.VMEM)] * 2,
        out_shape=[wide, wide, wide, block, block],
        compiler_params=pltpu.CompilerParams(vmem_limit_bytes=VMEM_BYTES),
        cost_estimate=pl.CostEstimate(flops=400000000, bytes_accessed=12000000, transcendentals=600000),
        name="attend_first",
    )(place, proj, totals)


def later_kernel(offsets, place_ref, query_ref, key_ref, value_ref, own_ref, other_ref, rows_ref):
    starts = [pl.multiple_of(lax.rem(place_ref[0] + offset, CHIPS) * 128, 128) for offset in offsets]
    for tower in (0, 1):
        for kind in (0, 1):
            for at, start in enumerate(starts):
                rows_ref[tower, kind, 128 * at : 128 * at + 128, :] = query_ref[tower, kind, pl.ds(start, 128), :]

    def put(tower, kind, value):
        lanes = pl.ds(128 * kind, 128)
        for at in range(len(offsets)):
            own, other = split_block(value[128 * at : 128 * at + 128], place_ref[1])
            own_ref[at, tower, :, lanes] = own
            other_ref[at, tower, :, lanes] = other

    attend_block(rows_ref, key_ref, value_ref, slice(None), put)


def attend_later(offsets, place, query, key, value):
    block = jax.ShapeDtypeStruct((len(offsets), 2, 64, 256), jnp.bfloat16)
    return pl.pallas_call(
        functools.partial(later_kernel, offsets),
        in_specs=[pl.BlockSpec(memory_space=pltpu.SMEM)] + [pl.BlockSpec(memory_space=pltpu.VMEM)] * 3,
        out_shape=[block, block],
        scratch_shapes=[pltpu.VMEM((2, 2, 128 * len(offsets), 256), jnp.bfloat16)],
        compiler_params=pltpu.CompilerParams(vmem_limit_bytes=VMEM_BYTES),
        cost_estimate=pl.CostEstimate(
            flops=500000000 * len(offsets), bytes_accessed=8000000, transcendentals=500000 * len(offsets)
        ),
        name="attend_later",
    )(place, query, key, value)


def shards(x_video, x_audio, len_video, len_audio, in_video, in_audio, out_video, out_audio):
    spot = lax.axis_index("sp")
    chip, core = spot // 2, spot % 2
    plane = lax.axis_index("fsdp")
    own = layer_norms(x_video[0], x_audio[0])
    shard = jnp.concatenate([in_video.transpose(1, 0, 2), out_video.transpose(0, 2, 1), out_audio.transpose(0, 2, 1)])
    wide = lax.all_gather(shard, "fsdp", axis=1, tiled=True)
    pieces = gather_plane(in_audio.transpose(1, 0, 2))

    blocks, far_v, far_a = gather_tokens(own)
    near = [b for o in NEAR for b in (blocks[o], other_core(blocks[o]))]
    far = [far_v, other_core(far_v), far_a, other_core(far_a)]
    offset, side = jnp.arange(CHIPS), jnp.arange(2)
    token_rows = (chip + offset[:, None]) % CHIPS * 128 + (side[None] ^ core) * 64
    x_places, y_places = jnp.array([0, -1, 1, 2]), jnp.array([0, -1, 2, 1])
    weight_rows = ((plane // 4 + x_places[:, None]) % 4 * 4 + (plane % 4 + y_places[None]) % 4) * ROWS
    rows = jnp.concatenate([token_rows.reshape(16), weight_rows.reshape(16)]).astype(jnp.int32)
    proj, squares = project(rows, near, far, wide, pieces)

    wide_out = wide[6:].transpose(0, 2, 1).reshape(2, 256, 3072)
    wide_out = jnp.concatenate([wide_out, other_core(wide_out)], axis=1)

    totals = over_heads(squares)
    place = jnp.stack([chip, core, len_video[0], len_audio[0]]).astype(jnp.int32)
    query, key, value, *first = attend_first(place, proj, totals)
    blocks = {4: (first[0], other_core(first[1]))}
    for offsets in ((3, 5), (2, 6, 1, 7, 0)):
        own, other = attend_later(offsets, place, query, key, value)
        other = other_core(other)
        blocks.update({offset: (own[at], other[at]) for at, offset in enumerate(offsets)})

    def part(tower, offset):
        values = jnp.concatenate([block[tower] for block in blocks[offset]], axis=1)
        return jnp.dot(values, wide_out[tower], preferred_element_type=jnp.float32)

    def chain(tower, steps, direction):
        total = None
        for step in range(steps, 0, -1):
            term = part(tower, step if direction > 0 else CHIPS - step)
            if total is not None:
                term = term + total.astype(jnp.float32)
            total = along_z(term.astype(jnp.bfloat16), direction)
        return total.astype(jnp.float32)

    ys = []
    for tower, x in ((0, x_video), (1, x_audio)):
        ahead = chain(tower, 4 - tower, 1)
        behind = chain(tower, 3 + tower, -1)
        ys.append((x[0].astype(jnp.float32) + part(tower, 0) + ahead + behind)[None])
    return tuple(ys)


def solution(mesh):
    in_specs = (
        P("fsdp", "sp", None),
        P("fsdp", "sp", None),
        P("fsdp"),
        P("fsdp"),
        P("fsdp", None, "sp"),
        P("fsdp", None, "sp"),
        P(None, "sp", "fsdp"),
        P(None, "sp", "fsdp"),
    )
    out_specs = (P("fsdp", "sp", None), P("fsdp", "sp", None))
    return jax.shard_map(shards, mesh=mesh, in_specs=in_specs, out_specs=out_specs, check_vma=False)
```

```python
import jax
import jax.numpy as jnp
from jax import lax
from jax.experimental import pallas as pl
from jax.experimental.pallas import tpu as pltpu
from jax.sharding import PartitionSpec as P

HDIM = 128
INNER = 2048
EPS = 1e-06
CHIPS = 8
ROWS = 192
LOG2E = 1.4426950408889634
NEAR = (0, 7, 1, 6, 2, 5, 3)
VMEM_BYTES = 56 * 1024 * 1024


def along_z(value, step):
    return lax.ppermute(value, "sp", [(s, ((s // 2 + step) % CHIPS) * 2 + s % 2) for s in range(16)])


def other_core(value):
    return lax.ppermute(value, "sp", [(s, s ^ 1) for s in range(16)])


def along_x(value, step):
    return lax.ppermute(value, "fsdp", [(f, ((f // 4 + step) % 4) * 4 + f % 4) for f in range(16)])


def along_y(value, step):
    return lax.ppermute(value, "fsdp", [(f, f // 4 * 4 + (f % 4 + step) % 4) for f in range(16)])


def norm_kernel(video_ref, audio_ref, out_ref):
    for at, ref in enumerate((video_ref, audio_ref)):
        values = ref[...].astype(jnp.float32)
        centre = jnp.mean(values, axis=-1, keepdims=True)
        values = values - centre
        spread = jnp.mean(values * values, axis=-1, keepdims=True)
        out_ref[pl.ds(64 * at, 64), :] = (values * lax.rsqrt(spread + EPS)).astype(jnp.bfloat16)


def layer_norms(video, audio):
    return pl.pallas_call(
        norm_kernel,
        out_shape=jax.ShapeDtypeStruct((128, 3072), jnp.bfloat16),
        cost_estimate=pl.CostEstimate(flops=128 * 3072 * 8, bytes_accessed=128 * 3072 * 4, transcendentals=128),
        name="layer_norms",
    )(video, audio)


def after(value, *others):
    return lax.optimization_barrier((value, *others))[0]


def gather_tokens(own):
    blocks = {0: own}
    ahead, behind = own, own
    for step in (1, 2, 3):
        ahead, behind = along_z(ahead, 1), along_z(behind, -1)
        blocks[CHIPS - step], blocks[step] = ahead, behind
    rows = own.shape[0] // 2
    return blocks, along_z(ahead[:rows], 1), along_z(behind[rows:], -1)


def gather_plane(own):
    up, down = along_y(own, 1), along_y(own, -1)
    half = own.shape[0] // 2
    far = jnp.concatenate([along_y(up[:half], 1), along_y(down[half:], -1)])
    line = jnp.stack([own, up, far, down])
    up, down = along_x(line, 1), along_x(line, -1)
    return line, up, down, along_x(up[:2], 1), along_x(down[2:], -1)


def project_kernel(row_ref, *refs):
    near, far, wide, pieces = refs[:14], refs[14:18], refs[18], refs[19:24]
    out_ref, square_ref, x_buf, w_buf, x_sem, w_sem = refs[24:]
    for tower in (0, 1):
        half = pl.ds(64 * tower, 64)
        for core in (0, 1):
            for at, place in enumerate(NEAR):
                row = pl.multiple_of(row_ref[2 * place + core], 64)
                pltpu.make_async_copy(
                    near[2 * at + core].at[half], x_buf.at[tower, pl.ds(row, 64)], x_sem.at[tower]
                ).start()
            row = pl.multiple_of(row_ref[8 + core], 64)
            pltpu.make_async_copy(
                far[2 * tower + core], x_buf.at[tower, pl.ds(row, 64)], x_sem.at[tower]
            ).start()
        if tower == 0:
            pltpu.make_async_copy(wide.at[pl.ds(0, 6)], w_buf.at[0], w_sem.at[0]).start()
        else:
            for place in range(16):
                row = pl.multiple_of(row_ref[16 + place], 64)
                group, inner = place // 4, place % 4
                if group == 3:
                    group, inner = (3, inner) if inner < 2 else (4, inner - 2)
                pltpu.make_async_copy(
                    pieces[group].at[inner], w_buf.at[1, :, pl.ds(row, ROWS)], w_sem.at[1]
                ).start()
    for tower in (0, 1):
        pltpu.make_async_copy(x_buf.at[tower], x_buf.at[tower], x_sem.at[tower]).wait()
        pltpu.make_async_copy(w_buf.at[tower], w_buf.at[tower], w_sem.at[tower]).wait()

        def tile(m, _):
            rows = pl.ds(pl.multiple_of(m * 512, 512), 512)
            total = None
            for k in range(0, 3072, 512):
                weights = jnp.concatenate([w_buf[tower, slot, k : k + 512] for slot in range(6)], axis=1)
                term = jnp.dot(x_buf[tower, rows, k : k + 512], weights, preferred_element_type=jnp.float32)
                total = term if total is None else total + term
            for slot in range(6):
                part = total[:, 128 * slot : 128 * slot + 128]
                out_ref[tower, slot, rows, :] = part
                if slot not in (2, 5):
                    line = 4 * tower + (0, 1, 0, 2, 3)[slot]
                    square_ref[line : line + 1, rows] = jnp.sum(
                        jnp.transpose(part * part), axis=0, keepdims=True
                    )
            return 0

        lax.fori_loop(0, 2, tile, 0)


def project(rows, near, far, wide, pieces):
    return pl.pallas_call(
        project_kernel,
        in_specs=[pl.BlockSpec(memory_space=pltpu.SMEM)] + [pl.BlockSpec(memory_space=pl.ANY)] * 24,
        scratch_shapes=[
            pltpu.VMEM((2, 1024, 3072), jnp.bfloat16),
            pltpu.VMEM((2, 6, 3072, 128), jnp.bfloat16),
            pltpu.SemaphoreType.DMA((2,)),
            pltpu.SemaphoreType.DMA((2,)),
        ],
        out_shape=[
            jax.ShapeDtypeStruct((2, 6, 1024, 128), jnp.float32),
            jax.ShapeDtypeStruct((8, 1024), jnp.float32),
        ],
        compiler_params=pltpu.CompilerParams(vmem_limit_bytes=VMEM_BYTES),
        cost_estimate=pl.CostEstimate(flops=9663676416, bytes_accessed=28000000, transcendentals=0),
        name="project",
    )(rows, *near, *far, wide, *pieces)


def over_heads(local):
    pair = local + other_core(local)
    two = pair + along_z(pair, 1)
    three = two + along_z(pair, -1)
    return three + along_z(three, 3) + along_z(two, -3)


def attend_block(query_ref, key_ref, value_ref, rows, put):
    for tower in (0, 1):
        for kind in (0, 1):
            other = tower ^ kind
            scores = lax.dot_general(
                query_ref[tower, kind, rows, :],
                key_ref[other, kind],
                (((1,), (1,)), ((), ())),
                preferred_element_type=jnp.float32,
            )
            top = jnp.max(scores, axis=-1, keepdims=True)
            expo = jnp.exp2((scores - top) * (LOG2E * HDIM ** (-0.5))).astype(jnp.bfloat16)
            result = jnp.dot(expo, value_ref[other, kind], preferred_element_type=jnp.float32)
            put(tower, kind, (result[:, :128] / result[:, 128:]).astype(jnp.bfloat16))


def split_block(value, core):
    low, high = value[:64], value[64:]
    return jnp.where(core == 0, low, high), jnp.where(core == 0, high, low)


def attend_kernel(place_ref, proj_ref, total_ref, own_ref, other_ref, query_ref, key_ref, value_ref):
    scales = jnp.transpose(lax.rsqrt(total_ref[...] / INNER + EPS))
    lane = lax.broadcasted_iota(jnp.int32, (1024, 128), 1)
    row = lax.broadcasted_iota(jnp.int32, (1024, 128), 0)
    one = jnp.where(lane == 0, 1.0, 0.0).astype(jnp.bfloat16)
    for tower in (0, 1):
        past = (lane == 0) & (row >= place_ref[2 + tower])
        mask = jnp.where(past, -1e30, 0.0).astype(jnp.bfloat16)
        for kind in (0, 1):
            line = 4 * tower + 2 * kind
            query = proj_ref[tower, 3 * kind] * scales[:, line : line + 1]
            key = proj_ref[tower, 3 * kind + 1] * scales[:, line + 1 : line + 2]
            query_ref[tower, kind, :, :128] = query.astype(jnp.bfloat16)
            query_ref[tower, kind, :, 128:] = one
            key_ref[tower, kind, :, :128] = key.astype(jnp.bfloat16)
            key_ref[tower, kind, :, 128:] = mask
            value_ref[tower, kind, :, :128] = proj_ref[tower, 3 * kind + 2].astype(jnp.bfloat16)
            value_ref[tower, kind, :, 128:] = jnp.ones((1024, 128), jnp.bfloat16)

    def body(i, _):
        def put(tower, kind, value):
            lanes = pl.ds(128 * kind, 128)
            for block in range(4):
                offset = lax.rem(4 * i + block + CHIPS - place_ref[0], CHIPS)
                own, other = split_block(value[128 * block : 128 * block + 128], place_ref[1])
                own_ref[offset, tower, :, lanes] = own
                other_ref[offset, tower, :, lanes] = other

        attend_block(query_ref, key_ref, value_ref, pl.ds(pl.multiple_of(i * 512, 512), 512), put)
        return 0

    lax.fori_loop(0, 2, body, 0)


def attend(place, proj, totals):
    block = jax.ShapeDtypeStruct((CHIPS, 2, 64, 256), jnp.bfloat16)
    return pl.pallas_call(
        attend_kernel,
        in_specs=[pl.BlockSpec(memory_space=pltpu.SMEM)] + [pl.BlockSpec(memory_space=pltpu.VMEM)] * 2,
        out_shape=[block, block],
        scratch_shapes=[pltpu.VMEM((2, 2, 1024, 256), jnp.bfloat16)] * 3,
        compiler_params=pltpu.CompilerParams(vmem_limit_bytes=VMEM_BYTES),
        cost_estimate=pl.CostEstimate(flops=4000000000, bytes_accessed=8000000, transcendentals=4000000),
        name="attend",
    )(place, proj, totals)


def shards(x_video, x_audio, len_video, len_audio, in_video, in_audio, out_video, out_audio):
    spot = lax.axis_index("sp")
    chip, core = spot // 2, spot % 2
    plane = lax.axis_index("fsdp")
    normed = layer_norms(x_video[0], x_audio[0])
    shard = jnp.concatenate([in_video.transpose(1, 0, 2), out_video.transpose(0, 2, 1), out_audio.transpose(0, 2, 1)])
    wide = lax.all_gather(shard, "fsdp", axis=1, tiled=True)
    pieces = gather_plane(in_audio.transpose(1, 0, 2))

    blocks, far_v, far_a = gather_tokens(normed)
    near = [b for o in NEAR for b in (blocks[o], other_core(blocks[o]))]
    far = [far_v, other_core(far_v), far_a, other_core(far_a)]
    offset, side = jnp.arange(CHIPS), jnp.arange(2)
    token_rows = (chip + offset[:, None]) % CHIPS * 128 + (side[None] ^ core) * 64
    x_places, y_places = jnp.array([0, -1, 1, 2]), jnp.array([0, -1, 2, 1])
    weight_rows = ((plane // 4 + x_places[:, None]) % 4 * 4 + (plane % 4 + y_places[None]) % 4) * ROWS
    rows = jnp.concatenate([token_rows.reshape(16), weight_rows.reshape(16)]).astype(jnp.int32)
    proj, squares = project(rows, near, far, wide, pieces)

    wide_out = wide[6:].transpose(0, 2, 1).reshape(2, 256, 3072)
    wide_out = jnp.concatenate([wide_out, other_core(wide_out)], axis=1)

    totals = over_heads(squares)
    place = jnp.stack([chip, core, len_video[0], len_audio[0]]).astype(jnp.int32)
    own, other = attend(place, proj, totals)
    other = other_core(other)

    def part(tower, offset):
        values = jnp.concatenate([own[offset, tower], other[offset, tower]], axis=1)
        return jnp.dot(values, wide_out[tower], preferred_element_type=jnp.float32)

    def chain(tower, steps, direction):
        total = None
        for step in range(steps, 0, -1):
            term = part(tower, step if direction > 0 else CHIPS - step)
            if total is not None:
                term = term + total.astype(jnp.float32)
            total = along_z(term.astype(jnp.bfloat16), direction)
        return total.astype(jnp.float32)

    ys = []
    for tower, x in ((0, x_video), (1, x_audio)):
        ahead = chain(tower, 4 - tower, 1)
        behind = chain(tower, 3 + tower, -1)
        ys.append((x[0].astype(jnp.float32) + part(tower, 0) + ahead + behind)[None])
    return tuple(ys)


def solution(mesh):
    in_specs = (
        P("fsdp", "sp", None),
        P("fsdp", "sp", None),
        P("fsdp"),
        P("fsdp"),
        P("fsdp", None, "sp"),
        P("fsdp", None, "sp"),
        P(None, "sp", "fsdp"),
        P(None, "sp", "fsdp"),
    )
    out_specs = (P("fsdp", "sp", None), P("fsdp", "sp", None))
    return jax.shard_map(shards, mesh=mesh, in_specs=in_specs, out_specs=out_specs, check_vma=False)
```

```python
import functools

import jax
import jax.numpy as jnp
from jax import lax
from jax.experimental import pallas as pl
from jax.experimental.pallas import tpu as pltpu
from jax.sharding import PartitionSpec as P

HDIM = 128
INNER = 2048
EPS = 1e-06
CHIPS = 8
ROWS = 192
LOG2E = 1.4426950408889634
NEAR = (0, 7, 1, 6, 2, 5, 3)
VMEM_BYTES = 56 * 1024 * 1024


def along_z(value, step):
    return lax.ppermute(value, "sp", [(s, ((s // 2 + step) % CHIPS) * 2 + s % 2) for s in range(16)])


def other_core(value):
    return lax.ppermute(value, "sp", [(s, s ^ 1) for s in range(16)])


def along_x(value, step):
    return lax.ppermute(value, "fsdp", [(f, ((f // 4 + step) % 4) * 4 + f % 4) for f in range(16)])


def along_y(value, step):
    return lax.ppermute(value, "fsdp", [(f, f // 4 * 4 + (f % 4 + step) % 4) for f in range(16)])


def norm_kernel(video_ref, audio_ref, out_ref):
    for at, ref in enumerate((video_ref, audio_ref)):
        values = ref[...].astype(jnp.float32)
        centre = jnp.mean(values, axis=-1, keepdims=True)
        values = values - centre
        spread = jnp.mean(values * values, axis=-1, keepdims=True)
        out_ref[pl.ds(64 * at, 64), :] = (values * lax.rsqrt(spread + EPS)).astype(jnp.bfloat16)


def layer_norms(video, audio):
    return pl.pallas_call(
        norm_kernel,
        out_shape=jax.ShapeDtypeStruct((128, 3072), jnp.bfloat16),
        cost_estimate=pl.CostEstimate(flops=128 * 3072 * 8, bytes_accessed=128 * 3072 * 4, transcendentals=128),
        name="layer_norms",
    )(video, audio)


def after(value, *others):
    return lax.optimization_barrier((value, *others))[0]


def together(*values):
    return lax.optimization_barrier(values)


def gather(own, weight):
    own, weight = together(own, weight)
    rows = own.shape[0] // 2
    ahead, behind, y_up, y_down, y_far = together(
        along_z(own, 1), along_z(own, -1), along_y(weight, 1), along_y(weight, -1), along_y(weight, 2)
    )
    blocks = [own, ahead, behind]
    first, second = jnp.stack([weight, y_up]), jnp.stack([y_far, y_down])
    x_up, x_down, ahead, behind = together(
        along_x(first, 1), along_x(first, -1), along_z(ahead, 1), along_z(behind, -1)
    )
    blocks += [ahead, behind]
    x_up2, x_down2, ahead, behind = together(
        along_x(second, 1), along_x(second, -1), along_z(ahead, 1), along_z(behind, -1)
    )
    blocks += [ahead, behind]
    *blocks, far_up, far_down = together(*blocks, x_up, x_down2)
    far_v, far_a = along_z(blocks[5][:rows], 1), along_z(blocks[6][rows:], -1)
    far_up, far_down = along_x(far_up, 1), along_x(far_down, -1)
    swapped = [other_core(block) for block in blocks]
    pieces = [weight, y_up, y_far, y_down] + [
        (array, at) for array in (x_up, x_up2, x_down, x_down2, far_up, far_down) for at in (0, 1)
    ]
    return blocks, swapped, (far_v, other_core(far_v), far_a, other_core(far_a)), pieces


def project_kernel(places, row_ref, *refs):
    near, far, wide = refs[:14], refs[14:18], refs[18]
    out_ref, square_ref, x_buf, w_buf, x_sem, w_sem = refs[-6:]
    pieces = [refs[19 + at] if index is None else refs[19 + at].at[index] for at, index in places]
    for tower in (0, 1):
        half = pl.ds(64 * tower, 64)
        for core in (0, 1):
            for at, place in enumerate(NEAR):
                row = pl.multiple_of(row_ref[2 * place + core], 64)
                pltpu.make_async_copy(
                    near[2 * at + core].at[half], x_buf.at[tower, pl.ds(row, 64)], x_sem.at[tower]
                ).start()
            row = pl.multiple_of(row_ref[8 + core], 64)
            pltpu.make_async_copy(
                far[2 * tower + core], x_buf.at[tower, pl.ds(row, 64)], x_sem.at[tower]
            ).start()
        if tower == 0:
            pltpu.make_async_copy(wide, w_buf.at[0], w_sem.at[0]).start()
        else:
            for place in range(16):
                row = pl.multiple_of(row_ref[16 + place], 64)
                pltpu.make_async_copy(
                    pieces[place], w_buf.at[1, :, pl.ds(row, ROWS)], w_sem.at[1]
                ).start()
    for tower in (0, 1):
        pltpu.make_async_copy(x_buf.at[tower], x_buf.at[tower], x_sem.at[tower]).wait()
        pltpu.make_async_copy(w_buf.at[tower], w_buf.at[tower], w_sem.at[tower]).wait()

        def tile(m, _):
            rows = pl.ds(pl.multiple_of(m * 512, 512), 512)
            total = None
            for k in range(0, 3072, 512):
                weights = jnp.concatenate([w_buf[tower, slot, k : k + 512] for slot in range(6)], axis=1)
                term = jnp.dot(x_buf[tower, rows, k : k + 512], weights, preferred_element_type=jnp.float32)
                total = term if total is None else total + term
            for slot in range(6):
                part = total[:, 128 * slot : 128 * slot + 128]
                out_ref[tower, slot, rows, :] = part
                if slot not in (2, 5):
                    line = 4 * tower + (0, 1, 0, 2, 3)[slot]
                    square_ref[line : line + 1, rows] = jnp.sum(
                        jnp.transpose(part * part), axis=0, keepdims=True
                    )
            return 0

        lax.fori_loop(0, 2, tile, 0)


def project(rows, near, far, wide, pieces):
    arrays, places = [], []
    for piece in pieces:
        array, index = piece if isinstance(piece, tuple) else (piece, None)
        known = [at for at, other in enumerate(arrays) if other is array]
        places.append((known[0] if known else len(arrays), index))
        if not known:
            arrays.append(array)
    return pl.pallas_call(
        functools.partial(project_kernel, tuple(places)),
        in_specs=[pl.BlockSpec(memory_space=pltpu.SMEM)] + [pl.BlockSpec(memory_space=pl.ANY)] * (19 + len(arrays)),
        scratch_shapes=[
            pltpu.VMEM((2, 1024, 3072), jnp.bfloat16),
            pltpu.VMEM((2, 6, 3072, 128), jnp.bfloat16),
            pltpu.SemaphoreType.DMA((2,)),
            pltpu.SemaphoreType.DMA((2,)),
        ],
        out_shape=[
            jax.ShapeDtypeStruct((2, 6, 1024, 128), jnp.float32),
            jax.ShapeDtypeStruct((8, 1024), jnp.float32),
        ],
        compiler_params=pltpu.CompilerParams(vmem_limit_bytes=VMEM_BYTES),
        cost_estimate=pl.CostEstimate(flops=9663676416, bytes_accessed=28000000, transcendentals=0),
        name="project",
    )(rows, *near, *far, wide, *arrays)


def over_heads(local):
    pair = local + other_core(local)
    two = pair + along_z(pair, 1)
    three = two + along_z(pair, -1)
    return three + along_z(three, 3) + along_z(two, -3), three


def attend_block(query_ref, key_ref, value_ref, rows, put):
    for tower in (0, 1):
        for kind in (0, 1):
            other = tower ^ kind
            scores = lax.dot_general(
                query_ref[tower, kind, rows, :],
                key_ref[other, kind],
                (((1,), (1,)), ((), ())),
                preferred_element_type=jnp.float32,
            )
            top = jnp.max(scores, axis=-1, keepdims=True)
            expo = jnp.exp2((scores - top) * (LOG2E * HDIM ** (-0.5))).astype(jnp.bfloat16)
            result = jnp.dot(expo, value_ref[other, kind], preferred_element_type=jnp.float32)
            put(tower, kind, (result[:, :128] / result[:, 128:]).astype(jnp.bfloat16))


def split_block(value, core):
    low, high = value[:64], value[64:]
    return jnp.where(core == 0, low, high), jnp.where(core == 0, high, low)


def attend_kernel(place_ref, proj_ref, total_ref, own_ref, other_ref, query_ref, key_ref, value_ref):
    scales = jnp.transpose(lax.rsqrt(total_ref[...] / INNER + EPS))
    lane = lax.broadcasted_iota(jnp.int32, (1024, 128), 1)
    row = lax.broadcasted_iota(jnp.int32, (1024, 128), 0)
    one = jnp.where(lane == 0, 1.0, 0.0).astype(jnp.bfloat16)
    for tower in (0, 1):
        past = (lane == 0) & (row >= place_ref[2 + tower])
        mask = jnp.where(past, -1e30, 0.0).astype(jnp.bfloat16)
        for kind in (0, 1):
            line = 4 * tower + 2 * kind
            query = proj_ref[tower, 3 * kind] * scales[:, line : line + 1]
            key = proj_ref[tower, 3 * kind + 1] * scales[:, line + 1 : line + 2]
            query_ref[tower, kind, :, :128] = query.astype(jnp.bfloat16)
            query_ref[tower, kind, :, 128:] = one
            key_ref[tower, kind, :, :128] = key.astype(jnp.bfloat16)
            key_ref[tower, kind, :, 128:] = mask
            value_ref[tower, kind, :, :128] = proj_ref[tower, 3 * kind + 2].astype(jnp.bfloat16)
            value_ref[tower, kind, :, 128:] = jnp.ones((1024, 128), jnp.bfloat16)

    def body(i, _):
        def put(tower, kind, value):
            lanes = pl.ds(128 * kind, 128)
            for block in range(4):
                offset = lax.rem(4 * i + block + CHIPS - place_ref[0], CHIPS)
                own, other = split_block(value[128 * block : 128 * block + 128], place_ref[1])
                own_ref[offset, tower, :, lanes] = own
                other_ref[offset, tower, :, lanes] = other

        attend_block(query_ref, key_ref, value_ref, pl.ds(pl.multiple_of(i * 512, 512), 512), put)
        return 0

    lax.fori_loop(0, 2, body, 0)


def attend(place, proj, totals):
    block = jax.ShapeDtypeStruct((CHIPS, 2, 64, 256), jnp.bfloat16)
    return pl.pallas_call(
        attend_kernel,
        in_specs=[pl.BlockSpec(memory_space=pltpu.SMEM)] + [pl.BlockSpec(memory_space=pltpu.VMEM)] * 2,
        out_shape=[block, block],
        scratch_shapes=[pltpu.VMEM((2, 2, 1024, 256), jnp.bfloat16)] * 3,
        compiler_params=pltpu.CompilerParams(vmem_limit_bytes=VMEM_BYTES),
        cost_estimate=pl.CostEstimate(flops=4000000000, bytes_accessed=8000000, transcendentals=4000000),
        name="attend",
    )(place, proj, totals)


def shards(x_video, x_audio, len_video, len_audio, in_video, in_audio, out_video, out_audio):
    spot = lax.axis_index("sp")
    chip, core = spot // 2, spot % 2
    plane = lax.axis_index("fsdp")
    normed = layer_norms(x_video[0], x_audio[0])
    wide_v = lax.all_gather(in_video.transpose(1, 0, 2), "fsdp", axis=1, tiled=True)
    blocks, swapped, far, pieces = gather(normed, in_audio.transpose(1, 0, 2))
    outs = jnp.concatenate([out_video, out_audio]).transpose(0, 2, 1)
    wide_out = lax.all_gather(after(outs, blocks[1]), "fsdp", axis=1, tiled=True)
    near = [block for pair in zip(blocks, swapped) for block in pair]
    offset, side = jnp.arange(CHIPS), jnp.arange(2)
    token_rows = (chip + offset[:, None]) % CHIPS * 128 + (side[None] ^ core) * 64
    x_places, y_places = jnp.array([0, -1, 1, 2]), jnp.array([0, -1, 2, 1])
    weight_rows = ((plane // 4 + x_places[:, None]) % 4 * 4 + (plane % 4 + y_places[None]) % 4) * ROWS
    rows = jnp.concatenate([token_rows.reshape(16), weight_rows.reshape(16)]).astype(jnp.int32)
    proj, squares = project(rows, near, far, wide_v, pieces)

    totals, partial = over_heads(squares)
    wide_out = after(wide_out, partial).transpose(0, 2, 1).reshape(2, 256, 3072)
    wide_out = jnp.concatenate([wide_out, other_core(wide_out)], axis=1)
    place = jnp.stack([chip, core, len_video[0], len_audio[0]]).astype(jnp.int32)
    own, other = attend(place, proj, totals)
    other = other_core(other)

    def part(tower, offset):
        values = jnp.concatenate([own[offset, tower], other[offset, tower]], axis=1)
        return jnp.dot(values, wide_out[tower], preferred_element_type=jnp.float32)

    def chain(tower, steps, direction):
        total = None
        for step in range(steps, 0, -1):
            term = part(tower, step if direction > 0 else CHIPS - step)
            if total is not None:
                term = term + total.astype(jnp.float32)
            total = along_z(term.astype(jnp.bfloat16), direction)
        return total.astype(jnp.float32)

    ys = []
    for tower, x in ((0, x_video), (1, x_audio)):
        ahead = chain(tower, 4 - tower, 1)
        behind = chain(tower, 3 + tower, -1)
        ys.append((x[0].astype(jnp.float32) + part(tower, 0) + ahead + behind)[None])
    return tuple(ys)


def solution(mesh):
    in_specs = (
        P("fsdp", "sp", None),
        P("fsdp", "sp", None),
        P("fsdp"),
        P("fsdp"),
        P("fsdp", None, "sp"),
        P("fsdp", None, "sp"),
        P(None, "sp", "fsdp"),
        P(None, "sp", "fsdp"),
    )
    out_specs = (P("fsdp", "sp", None), P("fsdp", "sp", None))
    return jax.shard_map(shards, mesh=mesh, in_specs=in_specs, out_specs=out_specs, check_vma=False)
```

```python
import functools

import jax
import jax.numpy as jnp
from jax import lax
from jax.experimental import pallas as pl
from jax.experimental.pallas import tpu as pltpu
from jax.sharding import PartitionSpec as P

HDIM = 128
INNER = 2048
EPS = 1e-06
CHIPS = 8
ROWS = 192
LOG2E = 1.4426950408889634
NEAR = (0, 7, 1, 6, 2, 5, 3)
VMEM_BYTES = 56 * 1024 * 1024


def along_z(value, step):
    return lax.ppermute(value, "sp", [(s, ((s // 2 + step) % CHIPS) * 2 + s % 2) for s in range(16)])


def other_core(value):
    return lax.ppermute(value, "sp", [(s, s ^ 1) for s in range(16)])


def along_x(value, step):
    return lax.ppermute(value, "fsdp", [(f, ((f // 4 + step) % 4) * 4 + f % 4) for f in range(16)])


def along_y(value, step):
    return lax.ppermute(value, "fsdp", [(f, f // 4 * 4 + (f % 4 + step) % 4) for f in range(16)])


def norm_kernel(video_ref, audio_ref, out_ref):
    for at, ref in enumerate((video_ref, audio_ref)):
        values = ref[...].astype(jnp.float32)
        centre = jnp.mean(values, axis=-1, keepdims=True)
        values = values - centre
        spread = jnp.mean(values * values, axis=-1, keepdims=True)
        out_ref[pl.ds(64 * at, 64), :] = (values * lax.rsqrt(spread + EPS)).astype(jnp.bfloat16)


def layer_norms(video, audio):
    return pl.pallas_call(
        norm_kernel,
        out_shape=jax.ShapeDtypeStruct((128, 3072), jnp.bfloat16),
        cost_estimate=pl.CostEstimate(flops=128 * 3072 * 8, bytes_accessed=128 * 3072 * 4, transcendentals=128),
        name="layer_norms",
    )(video, audio)


def after(value, *others):
    return lax.optimization_barrier((value, *others))[0]


def together(*values):
    return lax.optimization_barrier(values)


def gather(own, weight, scalars):
    own, weight = together(own, weight)
    rows = own.shape[0] // 2
    y_up, y_down = along_y(weight, 1), along_y(weight, -1)
    ahead, behind, y_up, y_down, y_far, swap0, *scalars = together(
        along_z(own, 1),
        along_z(own, -1),
        y_up,
        y_down,
        along_y(weight, 2),
        other_core(after(own, y_up, y_down)),
        *scalars,
    )
    blocks = [own, ahead, behind]
    first, second = jnp.stack([weight, y_up]), jnp.stack([y_far, y_down])
    x_up, x_down, ahead, behind, swap1 = together(
        along_x(first, 1), along_x(first, -1), along_z(ahead, 1), along_z(behind, -1), other_core(ahead)
    )
    blocks += [ahead, behind]
    x_up2, x_down2, ahead, behind, swap2 = together(
        along_x(second, 1), along_x(second, -1), along_z(ahead, 1), along_z(behind, -1), other_core(blocks[2])
    )
    blocks += [ahead, behind]
    *blocks, far_up, far_down = together(*blocks, x_up, x_down2)
    far_v, far_a = along_z(blocks[5][:rows], 1), along_z(blocks[6][rows:], -1)
    far_up, far_down = along_x(far_up, 1), along_x(far_down, -1)
    swapped = [swap0, swap1, swap2, other_core(blocks[3])]
    swapped += [other_core(after(block, far_v, far_a)) for block in blocks[4:]]
    pieces = [weight, y_up, y_far, y_down] + [
        (array, at) for array in (x_up, x_up2, x_down, x_down2, far_up, far_down) for at in (0, 1)
    ]
    return blocks, swapped, (far_v, other_core(far_v), far_a, other_core(far_a)), pieces, scalars


def project_kernel(places, row_ref, *refs):
    near, far, wide = refs[:14], refs[14:18], refs[18]
    out_ref, square_ref, x_buf, w_buf, x_sem, w_sem = refs[-6:]
    pieces = [refs[19 + at] if index is None else refs[19 + at].at[index] for at, index in places]
    for tower in (0, 1):
        half = pl.ds(64 * tower, 64)
        for core in (0, 1):
            for at, place in enumerate(NEAR):
                row = pl.multiple_of(row_ref[2 * place + core], 64)
                pltpu.make_async_copy(
                    near[2 * at + core].at[half], x_buf.at[tower, pl.ds(row, 64)], x_sem.at[tower]
                ).start()
            row = pl.multiple_of(row_ref[8 + core], 64)
            pltpu.make_async_copy(
                far[2 * tower + core], x_buf.at[tower, pl.ds(row, 64)], x_sem.at[tower]
            ).start()
        if tower == 0:
            pltpu.make_async_copy(wide, w_buf.at[0], w_sem.at[0]).start()
        else:
            for place in range(16):
                row = pl.multiple_of(row_ref[16 + place], 64)
                pltpu.make_async_copy(
                    pieces[place], w_buf.at[1, :, pl.ds(row, ROWS)], w_sem.at[1]
                ).start()
    for tower in (0, 1):
        pltpu.make_async_copy(x_buf.at[tower], x_buf.at[tower], x_sem.at[tower]).wait()
        pltpu.make_async_copy(w_buf.at[tower], w_buf.at[tower], w_sem.at[tower]).wait()

        def tile(m, _):
            rows = pl.ds(pl.multiple_of(m * 512, 512), 512)
            total = None
            for k in range(0, 3072, 512):
                weights = jnp.concatenate([w_buf[tower, slot, k : k + 512] for slot in range(6)], axis=1)
                term = jnp.dot(x_buf[tower, rows, k : k + 512], weights, preferred_element_type=jnp.float32)
                total = term if total is None else total + term
            for slot in range(6):
                part = total[:, 128 * slot : 128 * slot + 128]
                out_ref[tower, slot, rows, :] = part
                if slot not in (2, 5):
                    line = 4 * tower + (0, 1, 0, 2, 3)[slot]
                    square_ref[line : line + 1, rows] = jnp.sum(
                        jnp.transpose(part * part), axis=0, keepdims=True
                    )
            return 0

        lax.fori_loop(0, 2, tile, 0)


def project(rows, near, far, wide, pieces):
    arrays, places = [], []
    for piece in pieces:
        array, index = piece if isinstance(piece, tuple) else (piece, None)
        known = [at for at, other in enumerate(arrays) if other is array]
        places.append((known[0] if known else len(arrays), index))
        if not known:
            arrays.append(array)
    return pl.pallas_call(
        functools.partial(project_kernel, tuple(places)),
        in_specs=[pl.BlockSpec(memory_space=pltpu.SMEM)] + [pl.BlockSpec(memory_space=pl.ANY)] * (19 + len(arrays)),
        scratch_shapes=[
            pltpu.VMEM((2, 1024, 3072), jnp.bfloat16),
            pltpu.VMEM((2, 6, 3072, 128), jnp.bfloat16),
            pltpu.SemaphoreType.DMA((2,)),
            pltpu.SemaphoreType.DMA((2,)),
        ],
        out_shape=[
            jax.ShapeDtypeStruct((2, 6, 1024, 128), jnp.float32),
            jax.ShapeDtypeStruct((8, 1024), jnp.float32),
        ],
        compiler_params=pltpu.CompilerParams(vmem_limit_bytes=VMEM_BYTES),
        cost_estimate=pl.CostEstimate(flops=9663676416, bytes_accessed=28000000, transcendentals=0),
        name="project",
    )(rows, *near, *far, wide, *arrays)


def over_heads(local):
    pair = local + other_core(local)
    two = pair + along_z(pair, 1)
    three = two + along_z(pair, -1)
    return three + along_z(three, 3) + along_z(two, -3)


def attend_block(query_ref, key_ref, value_ref, rows, put):
    for tower in (0, 1):
        for kind in (0, 1):
            other = tower ^ kind
            scores = lax.dot_general(
                query_ref[tower, kind, rows, :],
                key_ref[other, kind],
                (((1,), (1,)), ((), ())),
                preferred_element_type=jnp.float32,
            )
            top = jnp.max(scores, axis=-1, keepdims=True)
            expo = jnp.exp2((scores - top) * (LOG2E * HDIM ** (-0.5))).astype(jnp.bfloat16)
            result = jnp.dot(expo, value_ref[other, kind], preferred_element_type=jnp.float32)
            put(tower, kind, (result[:, :128] / result[:, 128:]).astype(jnp.bfloat16))


def split_block(value, core):
    low, high = value[:64], value[64:]
    return jnp.where(core == 0, low, high), jnp.where(core == 0, high, low)


def attend_kernel(place_ref, proj_ref, total_ref, own_ref, other_ref, query_ref, key_ref, value_ref):
    scales = jnp.transpose(lax.rsqrt(total_ref[...] / INNER + EPS))
    lane = lax.broadcasted_iota(jnp.int32, (1024, 128), 1)
    row = lax.broadcasted_iota(jnp.int32, (1024, 128), 0)
    one = jnp.where(lane == 0, 1.0, 0.0).astype(jnp.bfloat16)
    for tower in (0, 1):
        past = (lane == 0) & (row >= place_ref[2 + tower])
        mask = jnp.where(past, -1e30, 0.0).astype(jnp.bfloat16)
        for kind in (0, 1):
            line = 4 * tower + 2 * kind
            query = proj_ref[tower, 3 * kind] * scales[:, line : line + 1]
            key = proj_ref[tower, 3 * kind + 1] * scales[:, line + 1 : line + 2]
            query_ref[tower, kind, :, :128] = query.astype(jnp.bfloat16)
            query_ref[tower, kind, :, 128:] = one
            key_ref[tower, kind, :, :128] = key.astype(jnp.bfloat16)
            key_ref[tower, kind, :, 128:] = mask
            value_ref[tower, kind, :, :128] = proj_ref[tower, 3 * kind + 2].astype(jnp.bfloat16)
            value_ref[tower, kind, :, 128:] = jnp.ones((1024, 128), jnp.bfloat16)

    def put(tower, kind, value):
        lanes = pl.ds(128 * kind, 128)
        for block in range(CHIPS):
            offset = lax.rem(block + CHIPS - place_ref[0], CHIPS)
            own, other = split_block(value[128 * block : 128 * block + 128], place_ref[1])
            own_ref[offset, tower, :, lanes] = own
            other_ref[offset, tower, :, lanes] = other

    attend_block(query_ref, key_ref, value_ref, slice(None), put)


def attend(place, proj, totals):
    block = jax.ShapeDtypeStruct((CHIPS, 2, 64, 256), jnp.bfloat16)
    return pl.pallas_call(
        attend_kernel,
        in_specs=[pl.BlockSpec(memory_space=pltpu.SMEM)] + [pl.BlockSpec(memory_space=pltpu.VMEM)] * 2,
        out_shape=[block, block],
        scratch_shapes=[pltpu.VMEM((2, 2, 1024, 256), jnp.bfloat16)] * 3,
        compiler_params=pltpu.CompilerParams(vmem_limit_bytes=VMEM_BYTES),
        cost_estimate=pl.CostEstimate(flops=4000000000, bytes_accessed=8000000, transcendentals=4000000),
        name="attend",
    )(place, proj, totals)


def shards(x_video, x_audio, len_video, len_audio, in_video, in_audio, out_video, out_audio):
    spot = lax.axis_index("sp")
    chip, core = spot // 2, spot % 2
    plane = lax.axis_index("fsdp")
    normed = layer_norms(x_video[0], x_audio[0])
    offset, side = jnp.arange(CHIPS), jnp.arange(2)
    token_rows = (chip + offset[:, None]) % CHIPS * 128 + (side[None] ^ core) * 64
    x_places, y_places = jnp.array([0, -1, 1, 2]), jnp.array([0, -1, 2, 1])
    weight_rows = ((plane // 4 + x_places[:, None]) % 4 * 4 + (plane % 4 + y_places[None]) % 4) * ROWS
    rows = jnp.concatenate([token_rows.reshape(16), weight_rows.reshape(16)]).astype(jnp.int32)
    place = jnp.stack([chip, core, len_video[0], len_audio[0]]).astype(jnp.int32)
    wide_v = lax.all_gather(in_video.transpose(1, 0, 2), "fsdp", axis=1, tiled=True)
    blocks, swapped, far, pieces, (rows, place) = gather(normed, in_audio.transpose(1, 0, 2), (rows, place))
    outs = jnp.concatenate([out_video, out_audio]).transpose(0, 2, 1)
    wide_out = lax.all_gather(after(outs, blocks[1]), "fsdp", axis=1, tiled=True)
    near = [block for pair in zip(blocks, swapped) for block in pair]
    proj, squares = project(rows, near, far, wide_v, pieces)

    totals = over_heads(squares)
    wide_out = after(wide_out, totals).transpose(0, 2, 1).reshape(2, 256, 3072)
    wide_out = jnp.concatenate([wide_out, other_core(wide_out)], axis=1)
    own, other = attend(place, proj, totals)
    other = other_core(other)

    def part(tower, offset):
        values = jnp.concatenate([own[offset, tower], other[offset, tower]], axis=1)
        return jnp.dot(values, wide_out[tower], preferred_element_type=jnp.float32)

    def chain(tower, steps, direction):
        total = None
        for step in range(steps, 0, -1):
            term = part(tower, step if direction > 0 else CHIPS - step)
            if total is not None:
                term = term + total.astype(jnp.float32)
            total = along_z(term.astype(jnp.bfloat16), direction)
        return total.astype(jnp.float32)

    ys = []
    for tower, x in ((0, x_video), (1, x_audio)):
        ahead = chain(tower, 4 - tower, 1)
        behind = chain(tower, 3 + tower, -1)
        ys.append((x[0].astype(jnp.float32) + part(tower, 0) + ahead + behind)[None])
    return tuple(ys)


def solution(mesh):
    in_specs = (
        P("fsdp", "sp", None),
        P("fsdp", "sp", None),
        P("fsdp"),
        P("fsdp"),
        P("fsdp", None, "sp"),
        P("fsdp", None, "sp"),
        P(None, "sp", "fsdp"),
        P(None, "sp", "fsdp"),
    )
    out_specs = (P("fsdp", "sp", None), P("fsdp", "sp", None))
    return jax.shard_map(shards, mesh=mesh, in_specs=in_specs, out_specs=out_specs, check_vma=False)
```

```python
import functools

import jax
import jax.numpy as jnp
from jax import lax
from jax.experimental import pallas as pl
from jax.experimental.pallas import tpu as pltpu
from jax.sharding import PartitionSpec as P

HDIM = 128
INNER = 2048
EPS = 1e-06
CHIPS = 8
ROWS = 192
LOG2E = 1.4426950408889634
NEAR = (0, 7, 1, 6, 2, 5, 3)
VMEM_BYTES = 56 * 1024 * 1024


def along_z(value, step):
    return lax.ppermute(value, "sp", [(s, ((s // 2 + step) % CHIPS) * 2 + s % 2) for s in range(16)])


def other_core(value):
    return lax.ppermute(value, "sp", [(s, s ^ 1) for s in range(16)])


def along_x(value, step):
    return lax.ppermute(value, "fsdp", [(f, ((f // 4 + step) % 4) * 4 + f % 4) for f in range(16)])


def along_y(value, step):
    return lax.ppermute(value, "fsdp", [(f, f // 4 * 4 + (f % 4 + step) % 4) for f in range(16)])


def norm_kernel(video_ref, audio_ref, out_ref):
    for at, ref in enumerate((video_ref, audio_ref)):
        values = ref[...].astype(jnp.float32)
        centre = jnp.mean(values, axis=-1, keepdims=True)
        values = values - centre
        spread = jnp.mean(values * values, axis=-1, keepdims=True)
        out_ref[pl.ds(64 * at, 64), :] = (values * lax.rsqrt(spread + EPS)).astype(jnp.bfloat16)


def layer_norms(video, audio):
    return pl.pallas_call(
        norm_kernel,
        out_shape=jax.ShapeDtypeStruct((128, 3072), jnp.bfloat16),
        cost_estimate=pl.CostEstimate(flops=128 * 3072 * 8, bytes_accessed=128 * 3072 * 4, transcendentals=128),
        name="layer_norms",
    )(video, audio)


def after(value, *others):
    return lax.optimization_barrier((value, *others))[0]


def together(*values):
    return lax.optimization_barrier(values)


def gather(own, weight, scalars):
    own, weight = together(own, weight)
    rows = own.shape[0] // 2
    y_up, y_down = along_y(weight, 1), along_y(weight, -1)
    ahead, behind, y_up, y_down, y_far, swap0, *scalars = together(
        along_z(own, 1),
        along_z(own, -1),
        y_up,
        y_down,
        along_y(weight, 2),
        other_core(after(own, y_up, y_down)),
        *scalars,
    )
    blocks = [own, ahead, behind]
    first, second = jnp.stack([weight, y_up]), jnp.stack([y_far, y_down])
    x_up, x_down, ahead, behind, swap1 = together(
        along_x(first, 1), along_x(first, -1), along_z(ahead, 1), along_z(behind, -1), other_core(ahead)
    )
    blocks += [ahead, behind]
    x_up2, x_down2, ahead, behind, swap2 = together(
        along_x(second, 1), along_x(second, -1), along_z(ahead, 1), along_z(behind, -1), other_core(blocks[2])
    )
    blocks += [ahead, behind]
    *blocks, far_up, far_down = together(*blocks, x_up, x_down2)
    far_v, far_a = along_z(blocks[5][:rows], 1), along_z(blocks[6][rows:], -1)
    far_up, far_down = along_x(far_up, 1), along_x(far_down, -1)
    swapped = [swap0, swap1, swap2, other_core(blocks[3])]
    swapped += [other_core(after(block, far_v, far_a)) for block in blocks[4:]]
    pieces = [weight, y_up, y_far, y_down] + [
        (array, at) for array in (x_up, x_up2, x_down, x_down2, far_up, far_down) for at in (0, 1)
    ]
    return blocks, swapped, (far_v, other_core(far_v), far_a, other_core(far_a)), pieces, scalars


def project_kernel(places, row_ref, *refs):
    near, far, wide = refs[:14], refs[14:18], refs[18]
    out_ref, square_ref, x_buf, w_buf, x_sem, w_sem = refs[-6:]
    pieces = [refs[19 + at] if index is None else refs[19 + at].at[index] for at, index in places]
    for tower in (0, 1):
        half = pl.ds(64 * tower, 64)
        for core in (0, 1):
            for at, place in enumerate(NEAR):
                row = pl.multiple_of(row_ref[2 * place + core], 64)
                pltpu.make_async_copy(
                    near[2 * at + core].at[half], x_buf.at[tower, pl.ds(row, 64)], x_sem.at[tower]
                ).start()
            row = pl.multiple_of(row_ref[8 + core], 64)
            pltpu.make_async_copy(
                far[2 * tower + core], x_buf.at[tower, pl.ds(row, 64)], x_sem.at[tower]
            ).start()
        if tower == 0:
            pltpu.make_async_copy(wide, w_buf.at[0], w_sem.at[0]).start()
        else:
            for place in range(16):
                row = pl.multiple_of(row_ref[16 + place], 64)
                pltpu.make_async_copy(
                    pieces[place], w_buf.at[1, :, pl.ds(row, ROWS)], w_sem.at[1]
                ).start()
    for tower in (0, 1):
        pltpu.make_async_copy(x_buf.at[tower], x_buf.at[tower], x_sem.at[tower]).wait()
        pltpu.make_async_copy(w_buf.at[tower], w_buf.at[tower], w_sem.at[tower]).wait()

        def tile(m, _):
            rows = pl.ds(pl.multiple_of(m * 512, 512), 512)
            total = None
            for k in range(0, 3072, 512):
                weights = jnp.concatenate([w_buf[tower, slot, k : k + 512] for slot in range(6)], axis=1)
                term = jnp.dot(x_buf[tower, rows, k : k + 512], weights, preferred_element_type=jnp.float32)
                total = term if total is None else total + term
            for slot in range(6):
                part = total[:, 128 * slot : 128 * slot + 128]
                out_ref[tower, slot, rows, :] = part
                if slot not in (2, 5):
                    line = 4 * tower + (0, 1, 0, 2, 3)[slot]
                    square_ref[line : line + 1, rows] = jnp.sum(
                        jnp.transpose(part * part), axis=0, keepdims=True
                    )
            return 0

        lax.fori_loop(0, 2, tile, 0)


def project(rows, near, far, wide, pieces):
    arrays, places = [], []
    for piece in pieces:
        array, index = piece if isinstance(piece, tuple) else (piece, None)
        known = [at for at, other in enumerate(arrays) if other is array]
        places.append((known[0] if known else len(arrays), index))
        if not known:
            arrays.append(array)
    return pl.pallas_call(
        functools.partial(project_kernel, tuple(places)),
        in_specs=[pl.BlockSpec(memory_space=pltpu.SMEM)] + [pl.BlockSpec(memory_space=pl.ANY)] * (19 + len(arrays)),
        scratch_shapes=[
            pltpu.VMEM((2, 1024, 3072), jnp.bfloat16),
            pltpu.VMEM((2, 6, 3072, 128), jnp.bfloat16),
            pltpu.SemaphoreType.DMA((2,)),
            pltpu.SemaphoreType.DMA((2,)),
        ],
        out_shape=[
            jax.ShapeDtypeStruct((2, 6, 1024, 128), jnp.float32),
            jax.ShapeDtypeStruct((8, 1024), jnp.float32),
        ],
        compiler_params=pltpu.CompilerParams(vmem_limit_bytes=VMEM_BYTES),
        cost_estimate=pl.CostEstimate(flops=9663676416, bytes_accessed=28000000, transcendentals=0),
        name="project",
    )(rows, *near, *far, wide, *arrays)


def over_heads(local):
    pair = local + other_core(local)
    two = pair + along_z(pair, 1)
    three = two + along_z(pair, -1)
    up3 = along_z(three, 3)
    return three + up3 + along_z(two, -3), up3


def attend_block(query_ref, key_ref, value_ref, rows, put):
    for tower in (0, 1):
        for kind in (0, 1):
            other = tower ^ kind
            scores = lax.dot_general(
                query_ref[tower, kind, rows, :],
                key_ref[other, kind],
                (((1,), (1,)), ((), ())),
                preferred_element_type=jnp.float32,
            )
            top = jnp.max(scores, axis=-1, keepdims=True)
            expo = jnp.exp2((scores - top) * (LOG2E * HDIM ** (-0.5))).astype(jnp.bfloat16)
            result = jnp.dot(expo, value_ref[other, kind], preferred_element_type=jnp.float32)
            put(tower, kind, (result[:, :128] / result[:, 128:]).astype(jnp.bfloat16))


def split_block(value, core):
    low, high = value[:64], value[64:]
    return jnp.where(core == 0, low, high), jnp.where(core == 0, high, low)


def attend_kernel(place_ref, proj_ref, total_ref, own_ref, other_ref, query_ref, key_ref, value_ref):
    scales = jnp.transpose(lax.rsqrt(total_ref[...] / INNER + EPS))
    lane = lax.broadcasted_iota(jnp.int32, (1024, 128), 1)
    row = lax.broadcasted_iota(jnp.int32, (1024, 128), 0)
    one = jnp.where(lane == 0, 1.0, 0.0).astype(jnp.bfloat16)
    for tower in (0, 1):
        past = (lane == 0) & (row >= place_ref[2 + tower])
        mask = jnp.where(past, -1e30, 0.0).astype(jnp.bfloat16)
        for kind in (0, 1):
            line = 4 * tower + 2 * kind
            query = proj_ref[tower, 3 * kind] * scales[:, line : line + 1]
            key = proj_ref[tower, 3 * kind + 1] * scales[:, line + 1 : line + 2]
            query_ref[tower, kind, :, :128] = query.astype(jnp.bfloat16)
            query_ref[tower, kind, :, 128:] = one
            key_ref[tower, kind, :, :128] = key.astype(jnp.bfloat16)
            key_ref[tower, kind, :, 128:] = mask
            value_ref[tower, kind, :, :128] = proj_ref[tower, 3 * kind + 2].astype(jnp.bfloat16)
            value_ref[tower, kind, :, 128:] = jnp.ones((1024, 128), jnp.bfloat16)

    def put(tower, kind, value):
        lanes = pl.ds(128 * kind, 128)
        for block in range(CHIPS):
            offset = lax.rem(block + CHIPS - place_ref[0], CHIPS)
            own, other = split_block(value[128 * block : 128 * block + 128], place_ref[1])
            own_ref[offset, tower, :, lanes] = own
            other_ref[offset, tower, :, lanes] = other

    attend_block(query_ref, key_ref, value_ref, slice(None), put)


def attend(place, proj, totals):
    block = jax.ShapeDtypeStruct((CHIPS, 2, 64, 256), jnp.bfloat16)
    return pl.pallas_call(
        attend_kernel,
        in_specs=[pl.BlockSpec(memory_space=pltpu.SMEM)] + [pl.BlockSpec(memory_space=pltpu.VMEM)] * 2,
        out_shape=[block, block],
        scratch_shapes=[pltpu.VMEM((2, 2, 1024, 256), jnp.bfloat16)] * 3,
        compiler_params=pltpu.CompilerParams(vmem_limit_bytes=VMEM_BYTES),
        cost_estimate=pl.CostEstimate(flops=4000000000, bytes_accessed=8000000, transcendentals=4000000),
        name="attend",
    )(place, proj, totals)


def shards(x_video, x_audio, len_video, len_audio, in_video, in_audio, out_video, out_audio):
    spot = lax.axis_index("sp")
    chip, core = spot // 2, spot % 2
    plane = lax.axis_index("fsdp")
    normed = layer_norms(x_video[0], x_audio[0])
    offset, side = jnp.arange(CHIPS), jnp.arange(2)
    token_rows = (chip + offset[:, None]) % CHIPS * 128 + (side[None] ^ core) * 64
    x_places, y_places = jnp.array([0, -1, 1, 2]), jnp.array([0, -1, 2, 1])
    weight_rows = ((plane // 4 + x_places[:, None]) % 4 * 4 + (plane % 4 + y_places[None]) % 4) * ROWS
    rows = jnp.concatenate([token_rows.reshape(16), weight_rows.reshape(16)]).astype(jnp.int32)
    place = jnp.stack([chip, core, len_video[0], len_audio[0]]).astype(jnp.int32)
    wide_v = lax.all_gather(in_video.transpose(1, 0, 2), "fsdp", axis=1, tiled=True)
    blocks, swapped, far, pieces, (rows, place) = gather(normed, in_audio.transpose(1, 0, 2), (rows, place))
    outs = jnp.concatenate([out_video, out_audio]).transpose(0, 2, 1)
    wide_out = lax.all_gather(after(outs, blocks[1]), "fsdp", axis=1, tiled=True)
    near = [block for pair in zip(blocks, swapped) for block in pair]
    proj, squares = project(rows, near, far, wide_v, pieces)

    totals, arrived = over_heads(squares)
    wide_out = after(wide_out, arrived).transpose(0, 2, 1).reshape(2, 256, 3072)
    wide_out = jnp.concatenate([wide_out, other_core(wide_out)], axis=1)
    own, other = attend(place, proj, totals)
    other = other_core(other)

    def part(tower, offset):
        values = jnp.concatenate([own[offset, tower], other[offset, tower]], axis=1)
        return jnp.dot(values, wide_out[tower], preferred_element_type=jnp.float32)

    def chain(tower, steps, direction):
        total = None
        for step in range(steps, 0, -1):
            term = part(tower, step if direction > 0 else CHIPS - step)
            if total is not None:
                term = term + total.astype(jnp.float32)
            total = along_z(term.astype(jnp.bfloat16), direction)
        return total.astype(jnp.float32)

    ys = []
    for tower, x in ((0, x_video), (1, x_audio)):
        ahead = chain(tower, 4 - tower, 1)
        behind = chain(tower, 3 + tower, -1)
        ys.append((x[0].astype(jnp.float32) + part(tower, 0) + ahead + behind)[None])
    return tuple(ys)


def solution(mesh):
    in_specs = (
        P("fsdp", "sp", None),
        P("fsdp", "sp", None),
        P("fsdp"),
        P("fsdp"),
        P("fsdp", None, "sp"),
        P("fsdp", None, "sp"),
        P(None, "sp", "fsdp"),
        P(None, "sp", "fsdp"),
    )
    out_specs = (P("fsdp", "sp", None), P("fsdp", "sp", None))
    return jax.shard_map(shards, mesh=mesh, in_specs=in_specs, out_specs=out_specs, check_vma=False)
```
